32 devices in a mesh: region: 2 (over y), tile: 4 (over z), sub: 4 (over x, core).
Axes of the slice: x: 2, y: 2, z: 4, core: 2. Of those that a mesh axis runs over, the one named last changes fastest.
Arguments:
- observations: float32 [8, 65536], P(None, ('region', 'tile', 'sub')), parts along dimension 1, may hold values from -15 to 15
- coords: float32 [2, 65536], P(None, ('region', 'tile')), parts along dimension 1, may hold values from 0 to 71
- pairs: int32 [8, 48, 2], P(('region', 'tile')), parts along dimension 0, may hold values from 0 to 31, as said below
- pair_count: int32 [8], P(('region', 'tile')), parts along dimension 0, may hold values from 15 to 24, as said below
Outputs:
- solution: float32 [8, 65536], P(None, ('region', 'tile', 'sub')), parts along dimension 1
- residual: float32 [8, 65536], P(None, ('region', 'tile', 'sub')), parts along dimension 1
The draws below stay inside these ranges and needn't reach their ends.
There are 2 independent parts, one for each index of `region`. The reference program is written for one: setup_inputs(seed, part) draws one part's arguments, and reference() takes and returns one part's arrays. A program takes and returns all parts, laid end to end along the dimension named above; each array names one. Nothing has to cross between parts.
Inputs may be any that keep to these rules, and one draw needn't show every extreme that they name: In tile-row group g, slots 0 to pair_count[g] - 1 hold distinct pairs (i, j) with g * 8 <= i < (g + 1) * 8 and j one of i, i + 1, i + 2 below 32; every (i, i), and every (i, i + 1) with i + 1 < 32, is among them; the other slots hold (g * 8, g * 8). `pair_count`: some group has 24 live pairs.
All inputs are finite; a program needn't handle non-finite values.
Results may differ from the reference program's by a relative error of at most 0.0059.
The reference program's roundings to bfloat16 on the way count: a program that leaves them out, or rounds other values in their place, can miss the bound.
Values may be sent and summed in bfloat16 or wider, within the bound.
A program may use at most 64 MiB of HBM per device.

```python
import math
import jax
import jax.numpy as jnp
from jax import lax

TS = 1024
RHS = 8
TPG = 8
ITERS = 2
NT = 32
NPTS = 32768
SLOTS = 48


def far_flags(key):
    inner_key = jax.random.fold_in(key, 101)
    groups = NT // TPG
    key_keep, key_full = jax.random.split(inner_key)
    keep_far = jax.random.randint(key_keep, (groups, TPG), 0, 2)
    full_group = jax.random.randint(key_full, (), 0, groups - 1)
    group_ids = jnp.arange(groups, dtype=jnp.int32)[:, None]
    keep_far = jnp.where(group_ids == full_group, 1, keep_far)
    tile_ids = group_ids * TPG + jnp.arange(TPG, dtype=jnp.int32)[None, :]
    far_flag = jnp.where(tile_ids + 2 < NT, keep_far, 0).astype(jnp.int32)
    return (group_ids, tile_ids, far_flag)


def pattern(key):
    group_ids, tile_ids, far_flag = far_flags(key)
    groups = NT // TPG
    always = jnp.ones_like(tile_ids)
    near_flag = jnp.where(tile_ids + 1 < NT, 1, 0)
    kept_flag = jnp.stack([always, near_flag, far_flag], axis=2).reshape(groups, 3 * TPG)
    col_ids = jnp.stack([tile_ids, tile_ids + 1, tile_ids + 2], axis=2).reshape(groups, 3 * TPG)
    row_ids = jnp.stack([tile_ids, tile_ids, tile_ids], axis=2).reshape(groups, 3 * TPG)
    ranking = jnp.argsort(1 - kept_flag, axis=1, stable=True)
    row_sorted = jnp.take_along_axis(row_ids, ranking, axis=1)
    col_sorted = jnp.take_along_axis(col_ids, ranking, axis=1)
    counts = jnp.sum(kept_flag, axis=1)
    alive_slot = jnp.arange(3 * TPG, dtype=jnp.int32)[None, :] < counts[:, None]
    first_tile = group_ids * TPG
    row_sorted = jnp.where(alive_slot, row_sorted, first_tile)
    col_sorted = jnp.where(alive_slot, col_sorted, first_tile)
    filler = jnp.broadcast_to(first_tile, (groups, SLOTS - 3 * TPG))
    row_full = jnp.concatenate([row_sorted, filler], axis=1)
    col_full = jnp.concatenate([col_sorted, filler], axis=1)
    pair_table = jnp.stack([row_full, col_full], axis=2).astype(jnp.int32)
    return (pair_table, counts.astype(jnp.int32))


def draw_pairs(key, part):
    return pattern(key)[0]


def draw_pair_count(key, part):
    return pattern(key)[1]


def draw_coords(key, part):
    group_ids, tile_ids, far_flag = far_flags(key)
    key = jax.random.fold_in(key, 3)
    flags = far_flag.reshape(NT)
    short_tile = jnp.concatenate([jnp.zeros((1,), jnp.int32), flags[:-1]]).astype(jnp.int32)
    short_before = (jnp.cumsum(short_tile) - short_tile).astype(jnp.int32)
    tile_order = jnp.arange(NT, dtype=jnp.int32)
    base_units = (44 * tile_order - 23 * short_before).astype(jnp.int32)
    height_units = jnp.where(short_tile == 1, 21, 44).astype(jnp.int32)
    point_tile = jnp.arange(NPTS, dtype=jnp.int32) // TS
    base_point = jnp.take(base_units, point_tile)
    height_point = jnp.take(height_units, point_tile)
    key_across, key_along = jax.random.split(key)
    frac_across = jax.random.uniform(key_across, (NPTS,), jnp.float32)
    frac_raw = jax.random.uniform(key_along, (NPTS,), jnp.float32)
    frac_along = frac_raw * frac_raw
    across = float(TS // 16) * frac_across
    along = 0.05 * base_point.astype(jnp.float32) + 0.05 * height_point.astype(jnp.float32) * frac_along
    return jnp.stack([across, along])


def draw_observations(key, part):
    key = jax.random.fold_in(key, 5)
    key_noise, key_scale = jax.random.split(key)
    position = jnp.arange(NPTS, dtype=jnp.float32) / NPTS
    trend = jnp.sqrt(1.0 + 8.0 * position)[None, :]
    row_scale = jnp.exp(jax.random.uniform(key_scale, (RHS, 1), jnp.float32, 0.0, math.log(3.0)))
    noise = jnp.clip(jax.random.normal(key_noise, (RHS, NPTS), jnp.float32), -4.0, 4.0)
    return 0.4 * row_scale * trend * noise


def setup_inputs(seed: int = 0, part: int = 0) -> dict:
    keys = jax.random.split(jax.random.key(seed), 5)
    part_keys = jax.random.split(jax.random.fold_in(keys[4], part), 5)
    return {
        "observations": draw_observations(jax.random.fold_in(jax.random.fold_in(keys[4], part), 71), part),
        "coords": draw_coords(jax.random.fold_in(jax.random.fold_in(keys[4], part), 71), part),
        "pairs": draw_pairs(jax.random.fold_in(jax.random.fold_in(keys[4], part), 71), part),
        "pair_count": draw_pair_count(jax.random.fold_in(jax.random.fold_in(keys[4], part), 71), part),
    }


nugget = 1.0
taper_range = 2.0
matern_range = 4.0
sqrt_three = math.sqrt(3.0)

def covariance_tile(row_coords, col_coords):
    delta_x = row_coords[0][:, None] - col_coords[0][None, :]
    delta_y = row_coords[1][:, None] - col_coords[1][None, :]
    distance = jnp.sqrt(delta_x * delta_x + delta_y * delta_y)
    scaled = sqrt_three * distance / matern_range
    matern = (1.0 + scaled) * jnp.exp(-scaled)
    reach_ratio = distance / taper_range
    falloff = jnp.maximum(1.0 - reach_ratio, 0.0)
    taper_val = falloff * falloff * (1.0 + 0.5 * reach_ratio)
    return (matern * taper_val).astype(jnp.bfloat16)

def apply_operator(direction, coords, pairs, pair_count):
    rounded = direction.astype(jnp.bfloat16)
    slot_total = pairs.shape[1]
    flat_pairs = pairs.reshape(-1, 2)
    alive_slot = (jnp.arange(slot_total, dtype=jnp.int32)[None, :] < pair_count[:, None]).reshape(-1)

    def visit_pair(totals, item):
        pair_row, alive = item
        row_start = (pair_row[0] * TS).astype(jnp.int32)
        col_start = (pair_row[1] * TS).astype(jnp.int32)
        cov_tile = covariance_tile(lax.dynamic_slice_in_dim(coords, row_start, TS, 1), lax.dynamic_slice_in_dim(coords, col_start, TS, 1))
        row_vec = lax.dynamic_slice_in_dim(rounded, row_start, TS, 1)
        col_vec = lax.dynamic_slice_in_dim(rounded, col_start, TS, 1)
        row_part = jnp.dot(col_vec, cov_tile.T, preferred_element_type=jnp.float32)
        col_part = jnp.dot(row_vec, cov_tile, preferred_element_type=jnp.float32)
        weight = jnp.where(alive, 1.0, 0.0).astype(jnp.float32)
        cross = jnp.where(alive & (pair_row[0] != pair_row[1]), 1.0, 0.0).astype(jnp.float32)
        current = lax.dynamic_slice_in_dim(totals, row_start, TS, 1)
        totals = lax.dynamic_update_slice_in_dim(totals, current + weight * row_part, row_start, 1)
        current = lax.dynamic_slice_in_dim(totals, col_start, TS, 1)
        totals = lax.dynamic_update_slice_in_dim(totals, current + cross * col_part, col_start, 1)
        return (totals, None)
    totals, _ = lax.scan(visit_pair, jnp.zeros(direction.shape, jnp.float32), (flat_pairs, alive_slot))
    return nugget * direction + totals

def reference(observations, coords, pairs, pair_count):
    solution = jnp.zeros_like(observations)
    residual = observations
    direction = observations
    norm_now = lax.optimization_barrier(jnp.sum(residual * residual, axis=1))
    for sweep in range(ITERS):
        image_vec = apply_operator(direction, coords, pairs, pair_count)
        step_len = norm_now / lax.optimization_barrier(jnp.sum(direction * image_vec, axis=1))
        solution = solution + step_len[:, None] * direction
        residual = residual - step_len[:, None] * image_vec
        if sweep + 1 < ITERS:
            norm_next = lax.optimization_barrier(jnp.sum(residual * residual, axis=1))
            direction = residual + (norm_next / norm_now)[:, None] * direction
            norm_now = norm_next
    return (solution, residual)
```

```python
import functools
import math

import jax
import jax.numpy as jnp
from jax import lax
from jax.experimental import pallas as pl
from jax.experimental.pallas import tpu as pltpu
from jax.sharding import PartitionSpec as P

TS = 1024
PIECE = 256
STEPS = TS // PIECE
MESH = pl.DeviceIdType.MESH

LN2 = math.log(2.0)
SCALE = math.sqrt(3.0) / 4.0 / LN2
EDGE = 2.0 * SCALE
FOLD = 2.0**-EDGE / EDGE**2
B0 = 1.5 * (1.0 + EDGE * LN2) * FOLD
B1 = -(1.5 * LN2 + (1.0 + EDGE * LN2) / (2.0 * EDGE)) * FOLD
B2 = LN2 / (2.0 * EDGE) * FOLD


def covariance(xr, yr, xc, yc):
    dx = xr - xc
    dy = yr - yc
    square = jnp.maximum(dx * dx + dy * dy, 1e-30)
    w = jnp.maximum(EDGE - square * lax.rsqrt(square), 0.0)
    poly = (B2 * w + B1) * w + B0
    return ((w * w) * poly * jnp.exp2(w)).astype(jnp.bfloat16)


def kernel(nt, ns, tiles, obs, coords, pairs, count, x_out, r_out,
           win_c, row_c, win_r, win_q, vb, tot1, tot2, got1, got2, diag_c, full_c,
           part, sub1, tile1, sub2, tile2, mid, send_sem, recv_sem):
    own = tiles * TS
    nd = nt * ns
    tile_id = lax.axis_index("tile")
    sub_id = lax.axis_index("sub")
    me = tile_id * ns + sub_id
    halo = [(h, h // tiles, h % tiles) for h in (tiles, tiles + 1)]
    reach = (tiles + 1) // tiles

    def linear(offset):
        d = lax.rem(me + offset + nd, nd)
        return {"tile": lax.div(d, ns), "sub": lax.rem(d, ns)}

    def sub_peer(offset):
        return {"sub": lax.rem(sub_id + offset, ns)}

    def tile_peer(offset):
        return {"tile": lax.rem(tile_id + offset, nt)}

    barrier = pltpu.get_barrier_semaphore()
    greet = [linear(k) for k in range(1, reach + 1)] + [linear(-k) for k in range(1, reach + 1)]
    greet += [sub_peer(d) for d in range(1, ns)] + [tile_peer(d) for d in range(1, nt)]
    for device in greet:
        pl.semaphore_signal(barrier, inc=1, device_id=device, device_id_type=MESH)

    used = [0]

    def send(src, dst, device):
        at = used[0]
        used[0] += 1
        copy = pltpu.make_async_remote_copy(
            src_ref=src, dst_ref=dst, send_sem=send_sem.at[at], recv_sem=recv_sem.at[at],
            device_id=device, device_id_type=MESH)
        copy.start()
        return copy

    def tile_of(ref, t):
        return ref.at[:, t * TS:(t + 1) * TS]

    first = pl.multiple_of(sub_id * own, own)
    mine = coords[:, pl.ds(first, own)] * SCALE
    win_c[:, 0:own] = mine
    win_r[:, 0:own] = obs[...]
    row_c[...] = jnp.transpose(jnp.concatenate([mine] * 4, axis=0))
    vb[0:8, 0:own] = obs[...].astype(jnp.bfloat16)
    vb[8:16, :] = jnp.zeros((8, own + 2 * TS), jnp.bfloat16)
    tot1[...] = jnp.zeros_like(tot1)
    tot2[...] = jnp.zeros_like(tot2)

    slot = lax.broadcasted_iota(jnp.int32, (pairs.shape[0], 1), 0)
    alive = slot < count[0]
    pi, pj = pairs[:, 0:1], pairs[:, 1:2]

    def far_flag(o):
        i = me * tiles + o
        hit = (pi == i) & (pj == i + 2) & alive
        return jnp.max(jnp.where(hit, 1.0, 0.0), axis=0, keepdims=True)

    def near_flag(o):
        return jnp.where(me * tiles + o + 1 < nd * tiles, 1.0, 0.0).astype(jnp.float32)

    pl.semaphore_wait(barrier, len(greet))
    sent = []
    wait_c = [send(tile_of(win_c, o), tile_of(win_c, h), linear(-k)) for h, k, o in halo]
    wait_r = [send(tile_of(win_r, o), tile_of(win_r, h), linear(-k)) for h, k, o in halo]
    sent += wait_c + wait_r

    def fold(value):
        return value[0:8] + value[8:16]

    def contract(tot, o, h, rows, chunk, flag):
        at = pl.multiple_of(o * TS + rows, PIECE)
        here = vb[:, pl.ds(at, PIECE)]
        there = vb[:, h * TS:(h + 1) * TS]
        col = fold(jnp.dot(here, chunk, preferred_element_type=jnp.float32))
        row = fold(lax.dot_general(there, chunk, (((1,), (1,)), ((), ())),
                                   preferred_element_type=jnp.float32))
        if flag is not None:
            col, row = col * flag, row * flag
        tot[:, h * TS:(h + 1) * TS] += col
        tot[:, pl.ds(at, PIECE)] += row

    def cov_chunk(o, h, rows):
        at = pl.multiple_of(o * TS + rows, PIECE)
        xr, yr = row_c[pl.ds(at, PIECE), 0:1], row_c[pl.ds(at, PIECE), 1:2]
        xc, yc = win_c[0:1, h * TS:(h + 1) * TS], win_c[1:2, h * TS:(h + 1) * TS]
        return covariance(xr, yr, xc, yc)

    blocks = [(o, o + 1) for o in range(tiles)] + [(o, o + 2) for o in range(tiles)]
    local = [b for b, (o, h) in enumerate(blocks) if h < tiles]
    cross = [b for b, (o, h) in enumerate(blocks) if h >= tiles]
    flags = {}
    for b, (o, h) in enumerate(blocks):
        if h - o == 2:
            flags[b] = far_flag(o)
        else:
            flags[b] = near_flag(o) if h >= tiles else None

    def full_block(b, tot, build):
        o, h = blocks[b]

        def step(i, carry):
            rows = pl.multiple_of(i * PIECE, PIECE)
            if build:
                chunk = cov_chunk(o, h, rows)
                full_c[b, pl.ds(rows, PIECE), :] = chunk
            else:
                chunk = full_c[b, pl.ds(rows, PIECE), :]
            contract(tot, o, h, rows, chunk, flags[b])
            return carry

        lax.fori_loop(0, STEPS, step, 0)

    def diag_block(o, tot, build):
        for k in range(STEPS):
            for l in range(k, STEPS):
                rk = slice(o * TS + k * PIECE, o * TS + (k + 1) * PIECE)
                rl = slice(o * TS + l * PIECE, o * TS + (l + 1) * PIECE)
                ck, cl = slice(k * PIECE, (k + 1) * PIECE), slice(l * PIECE, (l + 1) * PIECE)
                if build:
                    chunk = covariance(row_c[rk, 0:1], row_c[rk, 1:2], win_c[0:1, rl], win_c[1:2, rl])
                    diag_c[o, ck, cl] = chunk
                else:
                    chunk = diag_c[o, ck, cl]
                tot[:, rl] += fold(jnp.dot(vb[:, rk], chunk, preferred_element_type=jnp.float32))
                if k != l:
                    tot[:, rk] += fold(lax.dot_general(
                        vb[:, rl], chunk, (((1,), (1,)), ((), ())), preferred_element_type=jnp.float32))

    def spread(partial, dst, peer, n):
        return [send(partial, dst.at[d - 1], peer(d)) for d in range(1, n)]

    def gathered(own_part, copies, dst):
        total = own_part
        for d, copy in enumerate(copies):
            copy.wait_recv()
            total = total + dst[d]
        return total

    for o in range(tiles - 1):
        diag_block(o, tot1, True)
    for b in local:
        full_block(b, tot1, True)
    for copy in wait_c + wait_r:
        copy.wait_recv()
    vb[0:8, own:] = win_r[:, own:].astype(jnp.bfloat16)
    for b in cross:
        full_block(b, tot1, True)
    wait_1 = [send(tile_of(tot1, h), got1.at[h - tiles], linear(k)) for h, k, o in halo]
    sent += wait_1
    diag_block(tiles - 1, tot1, True)
    for copy in wait_1:
        copy.wait_recv()

    r0 = win_r[:, 0:own]
    win_q[:, 0:own] = r0 + tot1[:, 0:own]
    for h, k, o in halo:
        mask = jnp.where(me >= k, 1.0, 0.0).astype(jnp.float32)
        win_q[:, o * TS:(o + 1) * TS] += got1[h - tiles] * mask
    wait_q = [send(tile_of(win_q, o), tile_of(win_q, h), linear(-k)) for h, k, o in halo]
    sent += wait_q
    q0 = win_q[:, 0:own]
    high = q0.astype(jnp.bfloat16)
    vb[0:8, 0:own] = high
    vb[8:16, 0:own] = (q0 - high.astype(jnp.float32)).astype(jnp.bfloat16)

    lane = lax.broadcasted_iota(jnp.int32, (8, 128), 1)
    rr = jnp.sum(r0 * r0, axis=1, keepdims=True)
    rq = jnp.sum(r0 * q0, axis=1, keepdims=True)
    qq = jnp.sum(q0 * q0, axis=1, keepdims=True)
    part[0] = jnp.where(lane == 0, rr, jnp.where(lane == 1, rq, qq))
    go_sub = spread(part.at[0], sub1, sub_peer, ns)
    sent += go_sub

    for o in range(tiles - 1):
        diag_block(o, tot2, False)
    for b in local:
        full_block(b, tot2, False)
    part[1] = gathered(part[0], go_sub, sub1)
    go_tile = spread(part.at[1], tile1, tile_peer, nt)
    sent += go_tile
    for copy in wait_q:
        copy.wait_recv()
    far_q = win_q[:, own:]
    high = far_q.astype(jnp.bfloat16)
    vb[0:8, own:] = high
    vb[8:16, own:] = (far_q - high.astype(jnp.float32)).astype(jnp.bfloat16)
    for b in cross:
        full_block(b, tot2, False)
    wait_2 = [send(tile_of(tot2, h), got2.at[h - tiles], linear(k)) for h, k, o in halo]
    sent += wait_2
    diag_block(tiles - 1, tot2, False)

    sums = gathered(part[1], go_tile, tile1)
    rr, rq, qq = sums[:, 0:1], sums[:, 1:2], sums[:, 2:3]
    alpha = rr / rq
    new = alpha * alpha * qq - rr
    beta = new / rr
    near = 1.0 + beta

    d_win = near * win_r[...] - alpha * win_q[...]
    t_win = near * tot1[...] - alpha * tot2[...]
    d_own = d_win[:, 0:own]
    bend = jnp.sum(d_win * t_win, axis=1, keepdims=True) + jnp.sum(d_own * d_own, axis=1, keepdims=True)
    part[2] = jnp.broadcast_to(bend, (8, 128))
    go_sub = spread(part.at[2], sub2, sub_peer, ns)
    sent += go_sub
    part[3] = gathered(part[2], go_sub, sub2)
    go_tile = spread(part.at[3], tile2, tile_peer, nt)
    sent += go_tile

    for copy in wait_2:
        copy.wait_recv()
    r0 = win_r[:, 0:own]
    q0 = win_q[:, 0:own]
    mid[0] = q0 + tot2[:, 0:own]
    for h, k, o in halo:
        mask = jnp.where(me >= k, 1.0, 0.0).astype(jnp.float32)
        mid[0, :, o * TS:(o + 1) * TS] += got2[h - tiles] * mask
    mid[0] = near * q0 - alpha * mid[0]
    mid[1] = r0 - alpha * q0
    mid[2] = near * r0 - alpha * q0
    bend = gathered(part[3], go_tile, tile2)[:, 0:1]
    step = new / bend
    x_out[...] = alpha * r0 + step * mid[2]
    r_out[...] = mid[1] - step * mid[0]
    for copy in sent:
        copy.wait_send()


def local(nt, ns, observations, coords, pairs, pair_count):
    own = observations.shape[1]
    tiles = own // TS
    window = own + 2 * TS
    f32 = jnp.float32
    copies = 10 + 2 * (ns - 1) + 2 * (nt - 1)
    out = jax.ShapeDtypeStruct(observations.shape, f32)
    vmem = pl.BlockSpec(memory_space=pltpu.VMEM)
    return pl.pallas_call(
        functools.partial(kernel, nt, ns, tiles),
        out_shape=(out, out),
        in_specs=[vmem, vmem, vmem, pl.BlockSpec(memory_space=pltpu.SMEM)],
        out_specs=(vmem, vmem),
        scratch_shapes=[
            pltpu.VMEM((2, window), f32),
            pltpu.VMEM((own, 8), f32),
            pltpu.VMEM((8, window), f32),
            pltpu.VMEM((8, window), f32),
            pltpu.VMEM((16, window), jnp.bfloat16),
            pltpu.VMEM((8, window), f32),
            pltpu.VMEM((8, window), f32),
            pltpu.VMEM((2, 8, TS), f32),
            pltpu.VMEM((2, 8, TS), f32),
            pltpu.VMEM((tiles, TS, TS), jnp.bfloat16),
            pltpu.VMEM((2 * tiles, TS, TS), jnp.bfloat16),
            pltpu.VMEM((4, 8, 128), f32),
            pltpu.VMEM((ns - 1, 8, 128), f32),
            pltpu.VMEM((nt - 1, 8, 128), f32),
            pltpu.VMEM((ns - 1, 8, 128), f32),
            pltpu.VMEM((nt - 1, 8, 128), f32),
            pltpu.VMEM((3, 8, own), f32),
            pltpu.SemaphoreType.DMA((copies,)),
            pltpu.SemaphoreType.DMA((copies,)),
        ],
        compiler_params=pltpu.CompilerParams(
            collective_id=0, has_side_effects=True, vmem_limit_bytes=48 * 1024 * 1024),
    )(observations, coords, pairs[0], pair_count)


def solution(mesh):
    in_specs = (
        P(None, ("region", "tile", "sub")),
        P(None, ("region", "tile")),
        P(("region", "tile"), None, None),
        P(("region", "tile")),
    )
    out_specs = (P(None, ("region", "tile", "sub")), P(None, ("region", "tile", "sub")))
    body = functools.partial(local, mesh.shape["tile"], mesh.shape["sub"])
    return jax.shard_map(body, mesh=mesh, in_specs=in_specs, out_specs=out_specs, check_vma=False)
```

```python
import functools
import math

import jax
import jax.numpy as jnp
from jax import lax
from jax.experimental import pallas as pl
from jax.experimental.pallas import tpu as pltpu
from jax.sharding import PartitionSpec as P

TS = 1024
PIECE = 256
STEPS = TS // PIECE
MESH = pl.DeviceIdType.MESH

LN2 = math.log(2.0)
SCALE = math.sqrt(3.0) / 4.0 / LN2
EDGE = 2.0 * SCALE
FOLD = 2.0**-EDGE / EDGE**2
B0 = 1.5 * (1.0 + EDGE * LN2) * FOLD
B1 = -(1.5 * LN2 + (1.0 + EDGE * LN2) / (2.0 * EDGE)) * FOLD
B2 = LN2 / (2.0 * EDGE) * FOLD


def covariance(xr, yr, xc, yc):
    dx = xr - xc
    dy = yr - yc
    square = jnp.maximum(dx * dx + dy * dy, 1e-30)
    w = jnp.maximum(EDGE - square * lax.rsqrt(square), 0.0)
    poly = (B2 * w + B1) * w + B0
    return ((w * w) * poly * jnp.exp2(w)).astype(jnp.bfloat16)


def kernel(nt, ns, tiles, obs, coords, pairs_in, count_in, x_out, r_out,
           c_in, pairs, count, win_c, row_c, win_r, win_q, vb, tot1, tot2, got1, got2, diag_c, full_c,
           part, gather1, mid, load_sem, send_sem, recv_sem):
    own = tiles * TS
    nd = nt * ns
    tile_id = lax.axis_index("tile")
    sub_id = lax.axis_index("sub")
    me = tile_id * ns + sub_id
    if tiles == 1:
        spans = [(TS, TS, 1, 0), (2 * TS, TS, 2, 0)]
    else:
        spans = [(own, 2 * TS, 1, 0)]
    direct = nd <= 16

    def linear(offset):
        d = lax.rem(me + offset + nd, nd)
        return {"tile": lax.div(d, ns), "sub": lax.rem(d, ns)}

    def sub_peer(offset):
        return {"sub": lax.rem(sub_id + offset, ns)}

    def tile_peer(offset):
        return {"tile": lax.rem(tile_id + offset, nt)}

    win_c[:, own:] = jnp.zeros((2, 2 * TS), jnp.float32)
    win_r[:, own:] = jnp.zeros((8, 2 * TS), jnp.float32)
    win_q[:, own:] = jnp.zeros((8, 2 * TS), jnp.float32)
    barrier = pltpu.get_barrier_semaphore()
    if direct:
        greet = [linear(d) for d in range(1, nd)]
    else:
        greet = [linear(k) for _, _, k, _ in spans] + [linear(-k) for _, _, k, _ in spans]
        greet += [sub_peer(d) for d in range(1, ns)] + [tile_peer(d) for d in range(1, nt)]
    for device in greet:
        pl.semaphore_signal(barrier, inc=1, device_id=device, device_id_type=MESH)

    first = pl.multiple_of(sub_id * own, own)
    loads = [
        pltpu.make_async_copy(coords.at[:, pl.ds(first, own)], c_in, load_sem.at[0]),
        pltpu.make_async_copy(obs, win_r.at[:, 0:own], load_sem.at[1]),
        pltpu.make_async_copy(pairs_in, pairs, load_sem.at[2]),
        pltpu.make_async_copy(count_in, count, load_sem.at[3]),
    ]
    for copy in loads:
        copy.start()

    used = [0]
    sent = []

    def send(src, dst, device, gives=None, takes=None):
        at = used[0]
        used[0] += 1
        copy = pltpu.make_async_remote_copy(
            src_ref=src, dst_ref=dst, send_sem=send_sem.at[at], recv_sem=recv_sem.at[at],
            device_id=device, device_id_type=MESH)

        def where(cond, act):
            if cond is None:
                act()
            else:
                pl.when(cond)(act)

        where(gives, copy.start)
        sent.append(lambda: where(gives, copy.wait_send))
        return lambda: where(takes, copy.wait_recv)

    def leftward(ref):
        return [send(ref.at[:, o:o + n], ref.at[:, h:h + n], linear(-k), me >= k, me + k < nd)
                for h, n, k, o in spans]

    def rightward(ref, dst):
        return [send(ref.at[:, h:h + n], dst.at[:, h - own:h - own + n], linear(k), me + k < nd, me >= k)
                for h, n, k, o in spans]

    def add_received(ref, got):
        for h, n, k, o in spans:
            ref[:, o:o + n] += jnp.where(me >= k, got[:, h - own:h - own + n], 0.0)

    tot1[...] = jnp.zeros_like(tot1)
    tot2[...] = jnp.zeros_like(tot2)
    vb[8:16, :] = jnp.zeros((8, own + 2 * TS), jnp.bfloat16)
    for copy in loads:
        copy.wait()

    mine = c_in[...] * SCALE
    win_c[:, 0:own] = mine
    row_c[...] = jnp.transpose(jnp.concatenate([mine] * 4, axis=0))
    vb[0:8, 0:own] = win_r[:, 0:own].astype(jnp.bfloat16)

    slot = lax.broadcasted_iota(jnp.int32, (1, pairs.shape[1]), 1)
    alive = slot < count[0]
    pi, pj = pairs[0:1, :], pairs[1:2, :]

    def far_flag(o):
        i = me * tiles + o
        hit = (pi == i) & (pj == i + 2) & alive
        return jnp.max(jnp.where(hit, 1.0, 0.0), axis=1, keepdims=True)

    def near_flag(o):
        return jnp.where(me * tiles + o + 1 < nd * tiles, 1.0, 0.0).astype(jnp.float32)

    def fold(value):
        return value[0:8] + value[8:16]

    def contract(tot, o, h, rows, chunk, flag):
        at = pl.multiple_of(o * TS + rows, PIECE)
        here = vb[:, pl.ds(at, PIECE)]
        there = vb[:, h * TS:(h + 1) * TS]
        col = fold(jnp.dot(here, chunk, preferred_element_type=jnp.float32))
        row = fold(lax.dot_general(there, chunk, (((1,), (1,)), ((), ())),
                                   preferred_element_type=jnp.float32))
        if flag is not None:
            col, row = col * flag, row * flag
        tot[:, h * TS:(h + 1) * TS] += col
        tot[:, pl.ds(at, PIECE)] += row

    def cov_chunk(o, h, rows):
        at = pl.multiple_of(o * TS + rows, PIECE)
        xr, yr = row_c[pl.ds(at, PIECE), 0:1], row_c[pl.ds(at, PIECE), 1:2]
        xc, yc = win_c[0:1, h * TS:(h + 1) * TS], win_c[1:2, h * TS:(h + 1) * TS]
        return covariance(xr, yr, xc, yc)

    blocks = [(o, o + 1) for o in range(tiles)] + [(o, o + 2) for o in range(tiles)]
    local = [b for b, (o, h) in enumerate(blocks) if h < tiles]
    cross = [b for b, (o, h) in enumerate(blocks) if h >= tiles]
    flags = {}
    for b, (o, h) in enumerate(blocks):
        if h - o == 2:
            flags[b] = far_flag(o)
        else:
            flags[b] = near_flag(o) if h >= tiles else None

    def full_block(b, tot, build):
        o, h = blocks[b]

        def step(i, carry):
            rows = pl.multiple_of(i * PIECE, PIECE)
            if build:
                chunk = cov_chunk(o, h, rows)
                full_c[b, pl.ds(rows, PIECE), :] = chunk
            else:
                chunk = full_c[b, pl.ds(rows, PIECE), :]
            contract(tot, o, h, rows, chunk, flags[b])
            return carry

        lax.fori_loop(0, STEPS, step, 0)

    def diag_block(o, tot, build):
        for k in range(STEPS):
            for l in range(k, STEPS):
                rk = slice(o * TS + k * PIECE, o * TS + (k + 1) * PIECE)
                rl = slice(o * TS + l * PIECE, o * TS + (l + 1) * PIECE)
                ck, cl = slice(k * PIECE, (k + 1) * PIECE), slice(l * PIECE, (l + 1) * PIECE)
                if build:
                    chunk = covariance(row_c[rk, 0:1], row_c[rk, 1:2], win_c[0:1, rl], win_c[1:2, rl])
                    diag_c[o, ck, cl] = chunk
                else:
                    chunk = diag_c[o, ck, cl]
                tot[:, rl] += fold(jnp.dot(vb[:, rk], chunk, preferred_element_type=jnp.float32))
                if k != l:
                    tot[:, rk] += fold(lax.dot_general(
                        vb[:, rl], chunk, (((1,), (1,)), ((), ())), preferred_element_type=jnp.float32))

    def all_sum(value, at, dst):
        part[at] = value
        if direct:
            waits = [send(part.at[at], dst.at[d - 1], linear(d)) for d in range(1, nd)]
            at_end = at
            first_slot = 0
        else:
            waits = [send(part.at[at], dst.at[d - 1], sub_peer(d)) for d in range(1, ns)]
            for d, wait in enumerate(waits):
                wait()
            total = part[at]
            for d in range(ns - 1):
                total = total + dst[d]
            at_end = at + 1
            part[at_end] = total
            first_slot = ns - 1
            waits = [send(part.at[at_end], dst.at[ns - 1 + d - 1], tile_peer(d)) for d in range(1, nt)]

        def end():
            total = part[at_end]
            for wait in waits:
                wait()
            for d in range(len(waits)):
                total = total + dst[first_slot + d]
            return total

        return end

    for o in range(tiles - 1):
        diag_block(o, tot1, True)
    pl.semaphore_wait(barrier, len(greet))
    waits = leftward(win_c) + leftward(win_r)
    for b in local:
        full_block(b, tot1, True)
    for wait in waits:
        wait()
    vb[0:8, own:] = win_r[:, own:].astype(jnp.bfloat16)
    for b in cross:
        full_block(b, tot1, True)
    waits = rightward(tot1, got1)
    diag_block(tiles - 1, tot1, True)
    for wait in waits:
        wait()

    r0 = win_r[:, 0:own]
    win_q[:, 0:own] = r0 + tot1[:, 0:own]
    add_received(win_q, got1)
    waits = leftward(win_q)
    q0 = win_q[:, 0:own]
    high = q0.astype(jnp.bfloat16)
    vb[0:8, 0:own] = high
    vb[8:16, 0:own] = (q0 - high.astype(jnp.float32)).astype(jnp.bfloat16)

    for o in range(tiles - 1):
        diag_block(o, tot2, False)
    for b in local:
        full_block(b, tot2, False)
    for wait in waits:
        wait()
    far_q = win_q[:, own:]
    high = far_q.astype(jnp.bfloat16)
    vb[0:8, own:] = high
    vb[8:16, own:] = (far_q - high.astype(jnp.float32)).astype(jnp.bfloat16)
    for b in cross:
        full_block(b, tot2, False)
    waits = rightward(tot2, got2)
    diag_block(tiles - 1, tot2, False)

    def along(value):
        return jnp.sum(value, axis=1, keepdims=True)

    r0, q0 = win_r[:, 0:own], win_q[:, 0:own]
    lane = lax.broadcasted_iota(jnp.int32, (8, 128), 1)
    message = jnp.zeros((8, 128), jnp.float32)
    for at, value in enumerate((along(r0 * r0), along(r0 * q0), along(q0 * q0),
                                along(win_r[...] * tot2[...]), along(win_q[...] * tot2[...]))):
        message = jnp.where(lane == at, value, message)
    sums = all_sum(message, 0, gather1)

    for wait in waits:
        wait()
    mid[...] = q0 + tot2[:, 0:own]
    add_received(mid, got2)
    sums = sums()
    rr, rq, qq = sums[:, 0:1], sums[:, 1:2], sums[:, 2:3]
    rp, qp = rq + sums[:, 3:4], qq + sums[:, 4:5]
    alpha = rr / rq
    new = alpha * alpha * qq - rr
    beta = new / rr
    near = 1.0 + beta
    bend = near * near * rq - near * alpha * (rp + qq) + alpha * alpha * qp
    step = new / bend
    r0, q0 = win_r[:, 0:own], win_q[:, 0:own]
    x_out[...] = (alpha + step * near) * r0 - (step * alpha) * q0
    r_out[...] = r0 - (alpha + step * near) * q0 + (step * alpha) * mid[...]
    for wait in sent:
        wait()


def local(nt, ns, observations, coords, pairs, pair_count):
    own = observations.shape[1]
    tiles = own // TS
    window = own + 2 * TS
    f32 = jnp.float32
    peers = nt * ns - 1 if nt * ns <= 16 else ns - 1 + nt - 1
    copies = 10 + peers
    out = jax.ShapeDtypeStruct(observations.shape, f32)
    vmem = pl.BlockSpec(memory_space=pltpu.VMEM)
    return pl.pallas_call(
        functools.partial(kernel, nt, ns, tiles),
        out_shape=(out, out),
        in_specs=[pl.BlockSpec(memory_space=pl.ANY)] * 4,
        out_specs=(vmem, vmem),
        scratch_shapes=[
            pltpu.VMEM((2, own), f32),
            pltpu.VMEM((2, pairs.shape[1]), jnp.int32),
            pltpu.SMEM((1,), jnp.int32),
            pltpu.VMEM((2, window), f32),
            pltpu.VMEM((own, 8), f32),
            pltpu.VMEM((8, window), f32),
            pltpu.VMEM((8, window), f32),
            pltpu.VMEM((16, window), jnp.bfloat16),
            pltpu.VMEM((8, window), f32),
            pltpu.VMEM((8, window), f32),
            pltpu.VMEM((8, 2 * TS), f32),
            pltpu.VMEM((8, 2 * TS), f32),
            pltpu.VMEM((tiles, TS, TS), jnp.bfloat16),
            pltpu.VMEM((2 * tiles, TS, TS), jnp.bfloat16),
            pltpu.VMEM((2, 8, 128), f32),
            pltpu.VMEM((peers, 8, 128), f32),
            pltpu.VMEM((8, own), f32),
            pltpu.SemaphoreType.DMA((4,)),
            pltpu.SemaphoreType.DMA((copies,)),
            pltpu.SemaphoreType.DMA((copies,)),
        ],
        compiler_params=pltpu.CompilerParams(
            collective_id=0, has_side_effects=True, vmem_limit_bytes=48 * 1024 * 1024),
    )(observations, coords, pairs[0].T, pair_count)


def solution(mesh):
    in_specs = (
        P(None, ("region", "tile", "sub")),
        P(None, ("region", "tile")),
        P(("region", "tile"), None, None),
        P(("region", "tile")),
    )
    out_specs = (P(None, ("region", "tile", "sub")), P(None, ("region", "tile", "sub")))
    body = functools.partial(local, mesh.shape["tile"], mesh.shape["sub"])
    return jax.shard_map(body, mesh=mesh, in_specs=in_specs, out_specs=out_specs, check_vma=False)
```

```python
import functools
import math

import jax
import jax.numpy as jnp
from jax import lax
from jax.experimental import pallas as pl
from jax.experimental.pallas import tpu as pltpu
from jax.sharding import PartitionSpec as P

TS = 1024
PIECE = 256
STEPS = TS // PIECE
MESH = pl.DeviceIdType.MESH

LN2 = math.log(2.0)
SCALE = math.sqrt(3.0) / 4.0 / LN2
EDGE = 2.0 * SCALE
FOLD = 2.0**-EDGE / EDGE**2
B0 = 1.5 * (1.0 + EDGE * LN2) * FOLD
B1 = -(1.5 * LN2 + (1.0 + EDGE * LN2) / (2.0 * EDGE)) * FOLD
B2 = LN2 / (2.0 * EDGE) * FOLD


def covariance(xr, yr, xc, yc):
    dx = xr - xc
    dy = yr - yc
    square = jnp.maximum(dx * dx + dy * dy, 1e-30)
    w = jnp.maximum(EDGE - square * lax.rsqrt(square), 0.0)
    poly = (B2 * w + B1) * w + B0
    return ((w * w) * poly * jnp.exp2(w)).astype(jnp.bfloat16)


def kernel(nt, ns, tiles, obs, coords, pairs_in, count_in, x_out, r_out,
           c_in, pairs, count, win_c, row_c, win_r, win_q, vb, tot1, tot2, got1, got2, diag_c, full_c,
           part, gather1, mid, load_sem, send_sem, recv_sem):
    own = tiles * TS
    nd = nt * ns
    tile_id = lax.axis_index("tile")
    sub_id = lax.axis_index("sub")
    me = tile_id * ns + sub_id
    if tiles == 1:
        spans = [(TS, TS, 1, 0), (2 * TS, TS, 2, 0)]
    else:
        spans = [(own, 2 * TS, 1, 0)]
    direct = nd <= 16

    def linear(offset):
        d = lax.rem(me + offset + nd, nd)
        return {"tile": lax.div(d, ns), "sub": lax.rem(d, ns)}

    def sub_peer(offset):
        return {"sub": lax.rem(sub_id + offset, ns)}

    def tile_peer(offset):
        return {"tile": lax.rem(tile_id + offset, nt)}

    win_c[:, own:] = jnp.zeros((2, 2 * TS), jnp.float32)
    win_r[:, own:] = jnp.zeros((8, 2 * TS), jnp.float32)
    win_q[:, own:] = jnp.zeros((8, 2 * TS), jnp.float32)
    barrier = pltpu.get_barrier_semaphore()
    if direct:
        greet = [linear(d) for d in range(1, nd)]
    else:
        greet = [linear(k) for _, _, k, _ in spans] + [linear(-k) for _, _, k, _ in spans]
        greet += [sub_peer(d) for d in range(1, ns)] + [tile_peer(d) for d in range(1, nt)]
    for device in greet:
        pl.semaphore_signal(barrier, inc=1, device_id=device, device_id_type=MESH)

    first = pl.multiple_of(sub_id * own, own)
    loads = [
        pltpu.make_async_copy(coords.at[:, pl.ds(first, own)], c_in, load_sem.at[0]),
        pltpu.make_async_copy(obs, win_r.at[:, 0:own], load_sem.at[1]),
        pltpu.make_async_copy(pairs_in, pairs, load_sem.at[2]),
        pltpu.make_async_copy(count_in, count, load_sem.at[3]),
    ]
    for copy in loads:
        copy.start()

    used = [0]
    sent = []

    def send(src, dst, device, gives=None, takes=None):
        at = used[0]
        used[0] += 1
        copy = pltpu.make_async_remote_copy(
            src_ref=src, dst_ref=dst, send_sem=send_sem.at[at], recv_sem=recv_sem.at[at],
            device_id=device, device_id_type=MESH)

        def where(cond, act):
            if cond is None:
                act()
            else:
                pl.when(cond)(act)

        where(gives, copy.start)
        sent.append(lambda: where(gives, copy.wait_send))
        return lambda: where(takes, copy.wait_recv)

    def leftward(ref):
        return [send(ref.at[:, o:o + n], ref.at[:, h:h + n], linear(-k), me >= k, me + k < nd)
                for h, n, k, o in spans]

    def rightward(ref, dst):
        return [send(ref.at[:, h:h + n], dst.at[:, h - own:h - own + n], linear(k), me + k < nd, me >= k)
                for h, n, k, o in spans]

    def add_received(ref, got):
        for h, n, k, o in spans:
            ref[:, o:o + n] += jnp.where(me >= k, got[:, h - own:h - own + n], 0.0)

    tot1[...] = jnp.zeros_like(tot1)
    tot2[...] = jnp.zeros_like(tot2)
    vb[8:16, :] = jnp.zeros((8, own + 2 * TS), jnp.bfloat16)
    for copy in loads:
        copy.wait()

    mine = c_in[...] * SCALE
    win_c[:, 0:own] = mine
    row_c[...] = jnp.transpose(jnp.concatenate([mine] * 4, axis=0))
    vb[0:8, 0:own] = win_r[:, 0:own].astype(jnp.bfloat16)

    slot = lax.broadcasted_iota(jnp.int32, (1, pairs.shape[1]), 1)
    alive = slot < count[0]
    pi, pj = pairs[0:1, :], pairs[1:2, :]

    def far_flag(o):
        i = me * tiles + o
        hit = (pi == i) & (pj == i + 2) & alive
        return jnp.max(jnp.where(hit, 1.0, 0.0), axis=1, keepdims=True)

    def near_flag(o):
        return jnp.where(me * tiles + o + 1 < nd * tiles, 1.0, 0.0).astype(jnp.float32)

    def fold(value):
        return value[0:8] + value[8:16]

    fars = [far_flag(o) for o in range(tiles)]
    nears = [near_flag(o) for o in range(tiles)]

    def flag_of(b):
        value = jnp.zeros((1, 1), jnp.float32)
        for at, flag in enumerate(nears + fars):
            value = jnp.where(b == at, flag, value)
        return value

    def full_blocks(tot, build, arrive):
        def step(b, carry):
            pl.when(b == tiles - 1)(arrive)
            o = lax.rem(b, tiles)
            h = o + 1 + lax.div(b, tiles)
            o_at, h_at = pl.multiple_of(o * TS, TS), pl.multiple_of(h * TS, TS)
            flag = flag_of(b)
            there = vb[:, pl.ds(h_at, TS)]
            xc, yc = win_c[0:1, pl.ds(h_at, TS)], win_c[1:2, pl.ds(h_at, TS)]
            col = jnp.zeros((16, TS), jnp.float32)
            for i in range(STEPS):
                rows = slice(i * PIECE, (i + 1) * PIECE)
                at = pl.multiple_of(o_at + i * PIECE, PIECE)
                if build:
                    chunk = covariance(row_c[pl.ds(at, PIECE), 0:1], row_c[pl.ds(at, PIECE), 1:2], xc, yc)
                    full_c[b, rows, :] = chunk
                else:
                    chunk = full_c[b, rows, :]
                col += jnp.dot(vb[:, pl.ds(at, PIECE)], chunk, preferred_element_type=jnp.float32)
                row = lax.dot_general(there, chunk, (((1,), (1,)), ((), ())),
                                      preferred_element_type=jnp.float32)
                tot[:, pl.ds(at, PIECE)] += fold(row) * flag
            tot[:, pl.ds(h_at, TS)] += fold(col) * flag
            return carry

        lax.fori_loop(0, 2 * tiles, step, 0)

    def diag_block(o, tot, build):
        for k in range(STEPS):
            for l in range(k, STEPS):
                rk = slice(o * TS + k * PIECE, o * TS + (k + 1) * PIECE)
                rl = slice(o * TS + l * PIECE, o * TS + (l + 1) * PIECE)
                ck, cl = slice(k * PIECE, (k + 1) * PIECE), slice(l * PIECE, (l + 1) * PIECE)
                if build:
                    chunk = covariance(row_c[rk, 0:1], row_c[rk, 1:2], win_c[0:1, rl], win_c[1:2, rl])
                    diag_c[o, ck, cl] = chunk
                else:
                    chunk = diag_c[o, ck, cl]
                tot[:, rl] += fold(jnp.dot(vb[:, rk], chunk, preferred_element_type=jnp.float32))
                if k != l:
                    tot[:, rk] += fold(lax.dot_general(
                        vb[:, rl], chunk, (((1,), (1,)), ((), ())), preferred_element_type=jnp.float32))

    def all_sum(value, at, dst):
        part[at] = value
        if direct:
            waits = [send(part.at[at], dst.at[d - 1], linear(d)) for d in range(1, nd)]
            at_end = at
            first_slot = 0
        else:
            waits = [send(part.at[at], dst.at[d - 1], sub_peer(d)) for d in range(1, ns)]
            for d, wait in enumerate(waits):
                wait()
            total = part[at]
            for d in range(ns - 1):
                total = total + dst[d]
            at_end = at + 1
            part[at_end] = total
            first_slot = ns - 1
            waits = [send(part.at[at_end], dst.at[ns - 1 + d - 1], tile_peer(d)) for d in range(1, nt)]

        def end():
            total = part[at_end]
            for wait in waits:
                wait()
            for d in range(len(waits)):
                total = total + dst[first_slot + d]
            return total

        return end

    for o in range(tiles - 1):
        diag_block(o, tot1, True)
    pl.semaphore_wait(barrier, len(greet))
    waits_r = leftward(win_c) + leftward(win_r)

    def arrive_r():
        for wait in waits_r:
            wait()
        vb[0:8, own:] = win_r[:, own:].astype(jnp.bfloat16)

    full_blocks(tot1, True, arrive_r)
    waits = rightward(tot1, got1)
    diag_block(tiles - 1, tot1, True)
    for wait in waits:
        wait()

    r0 = win_r[:, 0:own]
    win_q[:, 0:own] = r0 + tot1[:, 0:own]
    add_received(win_q, got1)
    waits_q = leftward(win_q)
    q0 = win_q[:, 0:own]
    high = q0.astype(jnp.bfloat16)
    vb[0:8, 0:own] = high
    vb[8:16, 0:own] = (q0 - high.astype(jnp.float32)).astype(jnp.bfloat16)

    for o in range(tiles - 1):
        diag_block(o, tot2, False)

    def arrive_q():
        for wait in waits_q:
            wait()
        far_q = win_q[:, own:]
        high = far_q.astype(jnp.bfloat16)
        vb[0:8, own:] = high
        vb[8:16, own:] = (far_q - high.astype(jnp.float32)).astype(jnp.bfloat16)

    full_blocks(tot2, False, arrive_q)
    waits = rightward(tot2, got2)
    diag_block(tiles - 1, tot2, False)

    def along(value):
        return jnp.sum(value, axis=1, keepdims=True)

    r0, q0 = win_r[:, 0:own], win_q[:, 0:own]
    lane = lax.broadcasted_iota(jnp.int32, (8, 128), 1)
    message = jnp.zeros((8, 128), jnp.float32)
    for at, value in enumerate((along(r0 * r0), along(r0 * q0), along(q0 * q0),
                                along(win_r[...] * tot2[...]), along(win_q[...] * tot2[...]))):
        message = jnp.where(lane == at, value, message)
    sums = all_sum(message, 0, gather1)

    for wait in waits:
        wait()
    mid[...] = q0 + tot2[:, 0:own]
    add_received(mid, got2)
    sums = sums()
    rr, rq, qq = sums[:, 0:1], sums[:, 1:2], sums[:, 2:3]
    rp, qp = rq + sums[:, 3:4], qq + sums[:, 4:5]
    alpha = rr / rq
    new = alpha * alpha * qq - rr
    beta = new / rr
    near = 1.0 + beta
    bend = near * near * rq - near * alpha * (rp + qq) + alpha * alpha * qp
    step = new / bend
    r0, q0 = win_r[:, 0:own], win_q[:, 0:own]
    x_out[...] = (alpha + step * near) * r0 - (step * alpha) * q0
    r_out[...] = r0 - (alpha + step * near) * q0 + (step * alpha) * mid[...]
    for wait in sent:
        wait()


def local(nt, ns, observations, coords, pairs, pair_count):
    own = observations.shape[1]
    tiles = own // TS
    window = own + 2 * TS
    f32 = jnp.float32
    peers = nt * ns - 1 if nt * ns <= 16 else ns - 1 + nt - 1
    copies = 10 + peers
    out = jax.ShapeDtypeStruct(observations.shape, f32)
    vmem = pl.BlockSpec(memory_space=pltpu.VMEM)
    return pl.pallas_call(
        functools.partial(kernel, nt, ns, tiles),
        out_shape=(out, out),
        in_specs=[pl.BlockSpec(memory_space=pl.ANY)] * 4,
        out_specs=(vmem, vmem),
        scratch_shapes=[
            pltpu.VMEM((2, own), f32),
            pltpu.VMEM((2, pairs.shape[1]), jnp.int32),
            pltpu.SMEM((1,), jnp.int32),
            pltpu.VMEM((2, window), f32),
            pltpu.VMEM((own, 8), f32),
            pltpu.VMEM((8, window), f32),
            pltpu.VMEM((8, window), f32),
            pltpu.VMEM((16, window), jnp.bfloat16),
            pltpu.VMEM((8, window), f32),
            pltpu.VMEM((8, window), f32),
            pltpu.VMEM((8, 2 * TS), f32),
            pltpu.VMEM((8, 2 * TS), f32),
            pltpu.VMEM((tiles, TS, TS), jnp.bfloat16),
            pltpu.VMEM((2 * tiles, TS, TS), jnp.bfloat16),
            pltpu.VMEM((2, 8, 128), f32),
            pltpu.VMEM((peers, 8, 128), f32),
            pltpu.VMEM((8, own), f32),
            pltpu.SemaphoreType.DMA((4,)),
            pltpu.SemaphoreType.DMA((copies,)),
            pltpu.SemaphoreType.DMA((copies,)),
        ],
        compiler_params=pltpu.CompilerParams(
            collective_id=0, has_side_effects=True, vmem_limit_bytes=48 * 1024 * 1024),
    )(observations, coords, pairs[0].T, pair_count)


def solution(mesh):
    in_specs = (
        P(None, ("region", "tile", "sub")),
        P(None, ("region", "tile")),
        P(("region", "tile"), None, None),
        P(("region", "tile")),
    )
    out_specs = (P(None, ("region", "tile", "sub")), P(None, ("region", "tile", "sub")))
    body = functools.partial(local, mesh.shape["tile"], mesh.shape["sub"])
    return jax.shard_map(body, mesh=mesh, in_specs=in_specs, out_specs=out_specs, check_vma=False)
```
